32 devices in a mesh: group: 8 (over z, x), local: 4 (over y, core).
Axes of the slice: x: 2, y: 2, z: 4, core: 2. Of those that a mesh axis runs over, the one named last changes fastest.
Arguments:
- tokens: bfloat16 [256, 3584], P(('group', 'local')), may hold values from -6 to 6
- routes: int32 [256, 8], P(('group', 'local')), may hold values from 0 to 31, as said below
- route_gates: float32 [256, 8], P(('group', 'local')), may hold values from 0.2 to 2
- gate_weight: bfloat16 [32, 3584, 1024], P(('group', 'local')), may hold values from -0.09375 to 0.09375
- up_weight: bfloat16 [32, 3584, 1024], P(('group', 'local')), may hold values from -0.09375 to 0.09375
Outputs:
- routed_hidden: bfloat16 [32, 128, 1024], P(('group', 'local'))
The draws below stay inside these ranges and needn't reach their ends.
Inputs may be any that keep to these rules, and one draw needn't show every extreme that they name: `routes`: each token names 8 different experts, lying in exactly 4 of the 8 expert groups of 4 consecutive experts; in each aligned block of 2 tokens every block of 4 consecutive experts is used by exactly one token, which names 2 of its experts.
All inputs are finite; a program needn't handle non-finite values.
Results may differ from the reference program's by a relative error of at most 0.012.
Values may be sent and summed in bfloat16 or wider, within the bound.
A program may use at most 64 MiB of HBM per device.

```python
import math
import jax
import jax.numpy as jnp
from jax import lax

D = 3584
FF = 1024
NEG = 8
EXP_MESH = 4
TOPG = 4
TOP = 8
SPLIT = 1
FF_DEV = 1024
EXPERTS = 32
QPG = 1
PQ = 1
MT = 4
PICKS = 2
TOKENS = 256
BLOCK = 2
ROWS = 128
N_GROUP = 8


def draw_routes(key, part):
    base_key = jax.random.fold_in(key, 11)
    key_groups, key_quarters, key_bias, key_favour, key_noise = jax.random.split(base_key, 5)
    block_count = TOKENS // BLOCK
    sets_each = QPG // PQ
    group_scores = jax.random.randint(key_groups, (block_count, NEG), 0, 2 ** 20) * NEG + jnp.arange(NEG, dtype=jnp.int32)[None, :]
    group_order = jnp.argsort(group_scores, axis=1).astype(jnp.int32)
    quarter_scores = jax.random.randint(key_quarters, (block_count, NEG, QPG), 0, 2 ** 20) * QPG + jnp.arange(QPG, dtype=jnp.int32)[None, None, :]
    quarter_order = jnp.argsort(quarter_scores, axis=2).astype(jnp.int32)
    set_index = jnp.arange(BLOCK, dtype=jnp.int32)[:, None] + BLOCK * jnp.arange(TOPG, dtype=jnp.int32)[None, :]
    position = set_index // sets_each
    part_index = set_index % sets_each
    group_of = group_order[:, position]
    quarter_rows = quarter_order[:, position]
    quarter_pick = part_index[:, :, None] * PQ + jnp.arange(PQ, dtype=jnp.int32)[None, None, :]
    quarter_pick = jnp.broadcast_to(quarter_pick[None], (block_count, BLOCK, TOPG, PQ))
    quarters = jnp.take_along_axis(quarter_rows, quarter_pick, axis=3)
    blocks_used = (group_of[:, :, :, None] * QPG + quarters).reshape(TOKENS, MT)
    candidates = blocks_used[:, :, None] * EXP_MESH + jnp.arange(EXP_MESH, dtype=jnp.int32)[None, None, :]
    expert_bias = jax.random.randint(key_bias, (EXPERTS,), 0, 3000)
    hot_expert = jax.random.randint(key_favour, (), 0, EXPERTS)
    expert_bias = expert_bias + jnp.where(jnp.arange(EXPERTS, dtype=jnp.int32) == hot_expert, 1000000, 0)
    noise_draw = jax.random.randint(key_noise, candidates.shape, 0, 3000)
    scores = (noise_draw + expert_bias[candidates]) * EXP_MESH + jnp.arange(EXP_MESH, dtype=jnp.int32)[None, None, :]
    _, picked = lax.top_k(scores, PICKS)
    chosen = jnp.take_along_axis(candidates, picked, axis=2)
    return chosen.reshape(TOKENS, TOP).astype(jnp.int32)


def shard_levels(key, extent, pieces, smallest, largest):
    loudness = 1.0
    for dim, blocks in pieces:
        heights = jax.random.uniform(jax.random.fold_in(jax.random.fold_in(key, 6), dim), (blocks,), jnp.float32, smallest / len(pieces), largest / len(pieces))
        loudness = loudness * jnp.repeat(jnp.exp(heights), extent[dim] // blocks).reshape((-1,) + (1,) * (len(extent) - 1 - dim))
    return loudness


def bell_draw(key, extent, width, most, cuts=(), held_as=jnp.bfloat16):
    entries = width * jax.random.normal(key, extent, jnp.float32)
    if cuts:
        entries = entries * shard_levels(key, extent, cuts, -0.22, 0.18)
    return jnp.clip(entries, -most, most).astype(held_as)


def setup_inputs(seed: int = 0) -> dict:
    key_of = jax.random.split(jax.random.key(seed), 6)
    tokens = bell_draw(key_of[0], (TOKENS, D), 1.0, 6.0, ((0, 32),))
    routes = draw_routes(jax.random.fold_in(key_of[5], 71), 0)
    route_gates = jnp.clip(jnp.exp(math.log(2.0) - 2.3025851 * jax.random.uniform(key_of[2], (TOKENS, TOP), jnp.float32) ** shard_levels(key_of[2], (TOKENS, TOP), ((0, 32),), -0.2, 0.2)), 0.2, 2.0)
    gate_weight = bell_draw(key_of[3], (EXPERTS * SPLIT, D, FF_DEV), D ** -0.5, 0.09375, ((0, 32),))
    up_weight = bell_draw(key_of[4], (EXPERTS * SPLIT, D, FF_DEV), D ** -0.5, 0.09375, ((0, 32),))
    return dict(tokens=tokens, routes=routes, route_gates=route_gates, gate_weight=gate_weight, up_weight=up_weight)


def one_group(group_index, tokens, routes, route_gates, gate_weight, up_weight):
    member = jnp.any(routes // EXP_MESH == group_index, axis=1)
    row_order = jnp.argsort(jnp.where(member, 0, 1).astype(jnp.int32), stable=True)[:ROWS]
    token_rows = tokens[row_order]
    chosen_routes = routes[row_order]
    chosen_gates = route_gates[row_order]
    pieces_out = []
    for slot_index in range(EXP_MESH):
        expert = group_index * EXP_MESH + slot_index
        weight = jnp.sum(jnp.where(chosen_routes == expert, chosen_gates, jnp.zeros_like(chosen_gates)), axis=1)
        start_block = (expert * SPLIT).astype(jnp.int32)
        gate_block = lax.dynamic_slice_in_dim(gate_weight, start_block, SPLIT, 0)
        up_block = lax.dynamic_slice_in_dim(up_weight, start_block, SPLIT, 0)
        gate_full = jnp.transpose(gate_block, (1, 0, 2)).reshape(D, FF)
        up_full = jnp.transpose(up_block, (1, 0, 2)).reshape(D, FF)
        pre_gate = jnp.dot(token_rows, gate_full, preferred_element_type=jnp.float32)
        pre_up = jnp.dot(token_rows, up_full, preferred_element_type=jnp.float32)
        hidden = (jax.nn.silu(pre_gate) * pre_up * weight[:, None]).astype(jnp.bfloat16)
        pieces_out.append(jnp.transpose(hidden.reshape(ROWS, SPLIT, FF_DEV), (1, 0, 2)))
    return jnp.concatenate(pieces_out, axis=0)


def reference(tokens, routes, route_gates, gate_weight, up_weight):
    def per_group(group_index):
        return one_group(group_index, tokens, routes, route_gates, gate_weight, up_weight)

    stacked = lax.map(per_group, jnp.arange(N_GROUP, dtype=jnp.int32))
    return stacked.reshape(EXPERTS * SPLIT, ROWS, FF_DEV)
```

```python
import functools

import jax
import jax.numpy as jnp
from jax import lax
from jax.experimental import pallas as pl
from jax.experimental.pallas import tpu as pltpu
from jax.sharding import PartitionSpec as P

NEG = 8
EXP_MESH = 4
TOPG = 4
TOP = 8
LANES = 128
ROW_TILE = 16
CORES = 2


def block_tokens(n_group):
    return n_group // (TOPG * min(TOP // TOPG, n_group // NEG))


def kernel(
    n_group,
    n_local,
    tok_ref,
    rt_ref,
    ga_ref,
    gw_hbm,
    uw_hbm,
    out_ref,
    stage,
    recv_a,
    send_b,
    x0,
    x1,
    x2,
    x3,
    wg,
    wu,
    acc_g,
    acc_u,
    w_sem,
    a_send,
    a_recv,
    b_send,
    b_recv,
    c_send,
    x1_recv,
    x2_recv,
    x3_recv,
):
    g = lax.axis_index("group")
    me = lax.axis_index("local")
    n_tok, depth = tok_ref.shape
    chunk = depth // n_local
    block = block_tokens(n_group)
    piece = n_local * n_tok // block
    rows = n_group * piece
    n_top = rt_ref.shape[1]

    core = lax.rem(me, CORES)
    l_core = me + 1 - 2 * core
    l_y = lax.rem(me + CORES, n_local)
    l_diag = lax.rem(l_core + CORES, n_local)

    barrier = pltpu.get_barrier_semaphore()
    for k in range(1, n_local):
        pl.semaphore_signal(
            barrier, inc=1, device_id={"local": lax.rem(me + k, n_local)}, device_id_type=pl.DeviceIdType.MESH
        )
    for k in range(1, n_group):
        pl.semaphore_signal(
            barrier, inc=1, device_id={"group": lax.rem(g + k, n_group)}, device_id_type=pl.DeviceIdType.MESH
        )

    loads = []
    for slot, part in enumerate((me, l_core, l_y, l_diag)):
        at = pl.ds(pl.multiple_of(part * chunk, LANES), chunk)
        for i, (src, dst) in enumerate(((gw_hbm, wg), (uw_hbm, wu))):
            load = pltpu.make_async_copy(src.at[0, at, :], dst.at[slot], w_sem.at[slot, i])
            load.start()
            loads.append(load)

    lane = lax.broadcasted_iota(jnp.int32, (n_tok, LANES), 1)
    m = lax.broadcasted_iota(jnp.int32, (n_tok, rows), 1)
    t = lax.broadcasted_iota(jnp.int32, (n_tok, rows), 0) + me * n_tok
    routes = rt_ref[...]
    gates = ga_ref[...]
    dense = jnp.zeros((n_tok, LANES), jnp.float32)
    member = jnp.zeros((n_tok, rows), jnp.float32)
    for k in range(n_top):
        r = routes[:, k : k + 1]
        dense = dense + jnp.where(lane == r, gates[:, k : k + 1], 0.0)
        member = jnp.where((r >= (m // piece) * EXP_MESH) & (r < (m // piece + 1) * EXP_MESH), 1.0, member)
    chosen = jnp.where(t // block == lax.rem(m, piece), member, 0.0)
    for j in range(n_local):
        stage[j, :, :chunk] = tok_ref[:, j * chunk : (j + 1) * chunk]
        stage[j, :, chunk : chunk + LANES] = dense.astype(jnp.bfloat16)
        stage[j, :, chunk + LANES :] = chosen.astype(jnp.bfloat16)
    recv_a[me] = stage[me]

    pl.semaphore_wait(barrier, n_local - 1 + n_group - 1)

    sends = []
    for k in range(1, n_local):
        to = lax.rem(me + k, n_local)
        copy = pltpu.make_async_remote_copy(
            src_ref=stage.at[to],
            dst_ref=recv_a.at[me],
            send_sem=a_send.at[k],
            recv_sem=a_recv.at[k],
            device_id={"local": to},
            device_id_type=pl.DeviceIdType.MESH,
        )
        copy.start()
        sends.append(copy)
    for copy in sends:
        copy.wait_recv()

    got = jnp.concatenate([recv_a[j].astype(jnp.float32) for j in range(n_local)], axis=0).astype(jnp.bfloat16)
    packed = lax.dot_general(
        got[:, chunk + LANES :],
        got[:, : chunk + LANES],
        (((0,), (0,)), ((), ())),
        preferred_element_type=jnp.float32,
    ).astype(jnp.bfloat16)
    send_b[...] = packed.reshape(n_group, piece, chunk + LANES)

    far_first = sorted(range(1, n_group), key=lambda k: -min(k, n_group - k))
    for k in far_first:
        to = lax.rem(g + k, n_group)
        copy = pltpu.make_async_remote_copy(
            src_ref=send_b.at[to],
            dst_ref=x0.at[g],
            send_sem=b_send.at[k],
            recv_sem=b_recv.at[k],
            device_id={"group": to},
            device_id_type=pl.DeviceIdType.MESH,
        )
        copy.start()
        sends.append(copy)
    x0[g] = send_b[g]

    def onward(src, dst, at, send, recv, to):
        copy = pltpu.make_async_remote_copy(
            src_ref=src,
            dst_ref=dst.at[at],
            send_sem=send,
            recv_sem=recv,
            device_id={"local": to},
            device_id_type=pl.DeviceIdType.MESH,
        )
        copy.start()
        sends.append(copy)
        return copy

    order = [0] + far_first[::-1]
    b_copy = dict(zip(far_first, sends[n_local - 1 :]))
    core_in, y_in, diag_in = [], [], []

    def forward(step):
        at = lax.rem(g + n_group - order[step], n_group)
        y_in[step].wait_recv()
        diag_in.append(onward(x2.at[at], x3, at, c_send.at[2, step], x3_recv.at[step], l_core))

    lag = 2
    for step, k in enumerate(order):
        if k:
            b_copy[k].wait_recv()
        at = lax.rem(g + n_group - k, n_group)
        src = x0.at[at, :, pl.ds(0, chunk)]
        y_in.append(onward(src, x2, at, c_send.at[1, step], x2_recv.at[step], l_y))
        core_in.append(onward(src, x1, at, c_send.at[0, step], x1_recv.at[step], l_core))
        if step >= lag:
            forward(step - lag)

    def rows_of(x):
        return x[:, :, :chunk].reshape(rows, chunk)

    def add(slot, x, first=False):
        for load in loads[2 * slot : 2 * slot + 2]:
            load.wait()
        a = rows_of(x)
        for w, acc in ((wg, acc_g), (wu, acc_u)):
            p = jnp.dot(a, w[slot], preferred_element_type=jnp.float32)
            acc[...] = p if first else acc[...] + p

    add(0, x0, True)
    for step in range(n_group - lag, n_group):
        forward(step)
    for copy in core_in:
        copy.wait_recv()
    add(1, x1)
    add(2, x2)
    for copy in diag_in:
        copy.wait_recv()
    for load in loads[6:8]:
        load.wait()

    expert = g * EXP_MESH + me // (n_local // EXP_MESH)
    gate_rows = x0[:, :, chunk:].reshape(rows, LANES).astype(jnp.float32)
    mine = lax.broadcasted_iota(jnp.int32, (rows, LANES), 1) == expert
    scale = jnp.sum(jnp.where(mine, gate_rows, 0.0), axis=1, keepdims=True)
    a = rows_of(x3)
    width = 256
    for n in range(0, out_ref.shape[2], width):
        at = slice(n, n + width)
        pg = acc_g[:, at] + jnp.dot(a, wg[3, :, at], preferred_element_type=jnp.float32)
        pu = acc_u[:, at] + jnp.dot(a, wu[3, :, at], preferred_element_type=jnp.float32)
        out_ref[0, :, at] = (pg / (1.0 + jnp.exp(-pg)) * pu * scale).astype(jnp.bfloat16)

    for copy in sends:
        copy.wait_send()


def fused(tokens, routes, route_gates, gate_weight, up_weight):
    n_group, n_local = lax.axis_size("group"), lax.axis_size("local")
    n_tok, depth = tokens.shape
    hidden = gate_weight.shape[-1]
    chunk = depth // n_local
    piece = n_local * n_tok // block_tokens(n_group)
    rows = n_group * piece
    bf16, f32 = jnp.bfloat16, jnp.float32
    vmem = pl.BlockSpec(memory_space=pltpu.VMEM)
    hbm = pl.BlockSpec(memory_space=pl.ANY)
    dma = pltpu.SemaphoreType.DMA
    return pl.pallas_call(
        functools.partial(kernel, n_group, n_local),
        out_shape=jax.ShapeDtypeStruct((1, rows, hidden), bf16),
        in_specs=[vmem, vmem, vmem, hbm, hbm],
        out_specs=vmem,
        scratch_shapes=[
            pltpu.VMEM((n_local, n_tok, chunk + LANES + rows), bf16),
            pltpu.VMEM((n_local, n_tok, chunk + LANES + rows), bf16),
            pltpu.VMEM((n_group, piece, chunk + LANES), bf16),
            pltpu.VMEM((n_group, piece, chunk + LANES), bf16),
            pltpu.VMEM((n_group, piece, chunk), bf16),
            pltpu.VMEM((n_group, piece, chunk), bf16),
            pltpu.VMEM((n_group, piece, chunk), bf16),
            pltpu.VMEM((n_local, chunk, hidden), bf16),
            pltpu.VMEM((n_local, chunk, hidden), bf16),
            pltpu.VMEM((rows, hidden), f32),
            pltpu.VMEM((rows, hidden), f32),
            dma((n_local, 2)),
            dma((n_local,)),
            dma((n_local,)),
            dma((n_group,)),
            dma((n_group,)),
            dma((3, n_group)),
            dma((n_group,)),
            dma((n_group,)),
            dma((n_group,)),
        ],
        compiler_params=pltpu.CompilerParams(
            collective_id=0, has_side_effects=True, vmem_limit_bytes=48 * 1024 * 1024
        ),
        cost_estimate=pl.CostEstimate(
            flops=4 * rows * depth * hidden,
            bytes_accessed=4 * depth * hidden + 2 * rows * hidden,
            transcendentals=rows * hidden,
        ),
    )(tokens, routes, route_gates, gate_weight, up_weight)


def staged(tokens, routes, route_gates, gate_weight, up_weight):
    n_group, n_local = lax.axis_size("group"), lax.axis_size("local")
    block = block_tokens(n_group)
    n_tok, depth = tokens.shape
    groups = jnp.arange(n_group, dtype=jnp.int32)
    member = jnp.any((routes // EXP_MESH)[:, :, None] == groups, axis=1).astype(jnp.bfloat16)
    packed = jnp.einsum(
        "ibg,ibd->gid",
        member.reshape(-1, block, n_group),
        tokens.reshape(-1, block, depth),
        preferred_element_type=jnp.float32,
    ).astype(jnp.bfloat16)
    experts = groups[:, None] * EXP_MESH + jnp.arange(EXP_MESH, dtype=jnp.int32)
    matches = (routes[:, :, None, None] == experts).astype(jnp.float32)
    dense = jnp.sum(route_gates[:, :, None, None] * matches, axis=1)
    gates = dense.reshape(-1, block, n_group, EXP_MESH).sum(axis=1).transpose(1, 0, 2).astype(jnp.bfloat16)

    def over(x):
        x = lax.all_to_all(x, "group", split_axis=0, concat_axis=0, tiled=True)
        x = lax.all_gather(x, "local", axis=1, tiled=True)
        return x.reshape(-1, x.shape[-1])

    x, scales = over(packed), over(gates).astype(jnp.float32)
    slot = lax.axis_index("local") // (n_local // EXP_MESH)
    mine = (jnp.arange(EXP_MESH, dtype=jnp.int32) == slot).astype(jnp.float32)
    scale = jnp.sum(scales * mine, axis=-1)[:, None]
    pre_gate = jnp.dot(x, gate_weight[0], preferred_element_type=jnp.float32)
    pre_up = jnp.dot(x, up_weight[0], preferred_element_type=jnp.float32)
    return (jax.nn.silu(pre_gate) * pre_up * scale).astype(jnp.bfloat16)[None]


def shards(tokens, routes, route_gates, gate_weight, up_weight):
    n_group, n_local = lax.axis_size("group"), lax.axis_size("local")
    piece = n_local * tokens.shape[0] // block_tokens(n_group)
    fits = (
        n_local == 2 * CORES
        and n_local % EXP_MESH == 0
        and tokens.shape[1] % (n_local * LANES) == 0
        and piece % ROW_TILE == 0
        and (n_group * piece) % LANES == 0
        and n_group * EXP_MESH <= LANES
        and gate_weight.shape[-1] % 256 == 0
    )
    plan = fused if fits else staged
    return plan(tokens, routes, route_gates, gate_weight, up_weight)


def solution(mesh):
    rows = P(("group", "local"), None)
    blocks = P(("group", "local"), None, None)
    return jax.shard_map(
        shards, mesh=mesh, in_specs=(rows, rows, rows, blocks, blocks), out_specs=blocks, check_vma=False
    )
```

```python
import functools

import jax
import jax.numpy as jnp
from jax import lax
from jax.experimental import pallas as pl
from jax.experimental.pallas import tpu as pltpu
from jax.sharding import PartitionSpec as P

NEG = 8
EXP_MESH = 4
TOPG = 4
TOP = 8
LANES = 128
ROW_TILE = 16
CORES = 2


def block_tokens(n_group):
    return n_group // (TOPG * min(TOP // TOPG, n_group // NEG))


def flip(index, bits):
    bit = 1
    while bit <= bits:
        if bits & bit:
            index = index + bit * (1 - 2 * lax.rem(index // bit, 2))
        bit *= 2
    return index


def kernel(
    n_group,
    n_local,
    tok_hbm,
    rt_hbm,
    ga_hbm,
    gw_hbm,
    uw_hbm,
    out_ref,
    tok_ref,
    rt_ref,
    ga_ref,
    stage,
    recv_a,
    send_b,
    x0,
    x1,
    x2,
    x3,
    wg,
    wu,
    acc_g,
    acc_u,
    in_sem,
    w_sem,
    a_send,
    a_recv,
    b_send,
    b_recv,
    c_send,
    x1_recv,
    x2_recv,
    x3_recv,
):
    g = lax.axis_index("group")
    me = lax.axis_index("local")
    n_tok, depth = tok_ref.shape
    chunk = depth // n_local
    block = block_tokens(n_group)
    piece = n_local * n_tok // block
    rows = n_group * piece
    n_top = rt_ref.shape[1]

    core = lax.rem(me, CORES)
    l_core = me + 1 - 2 * core
    l_y = lax.rem(me + CORES, n_local)
    l_diag = lax.rem(l_core + CORES, n_local)

    small = []
    for i, (src, dst) in enumerate(((tok_hbm, tok_ref), (rt_hbm, rt_ref), (ga_hbm, ga_ref))):
        small.append(pltpu.make_async_copy(src, dst, in_sem.at[i]))
        small[-1].start()

    barrier = pltpu.get_barrier_semaphore()
    for k in range(1, n_local):
        pl.semaphore_signal(
            barrier, inc=1, device_id={"local": lax.rem(me + k, n_local)}, device_id_type=pl.DeviceIdType.MESH
        )
    for k in range(1, n_group):
        pl.semaphore_signal(
            barrier, inc=1, device_id={"group": flip(g, k)}, device_id_type=pl.DeviceIdType.MESH
        )

    loads = []
    for slot, part in enumerate((me, l_core, l_y, l_diag)):
        at = pl.ds(pl.multiple_of(part * chunk, LANES), chunk)
        for i, (src, dst) in enumerate(((gw_hbm, wg), (uw_hbm, wu))):
            load = pltpu.make_async_copy(src.at[0, at, :], dst.at[slot], w_sem.at[slot, i])
            load.start()
            loads.append(load)

    for copy in small:
        copy.wait()
    lane = lax.broadcasted_iota(jnp.int32, (n_tok, LANES), 1)
    m = lax.broadcasted_iota(jnp.int32, (n_tok, rows), 1)
    t = lax.broadcasted_iota(jnp.int32, (n_tok, rows), 0) + me * n_tok
    routes = rt_ref[...]
    gates = ga_ref[...]
    dense = jnp.zeros((n_tok, LANES), jnp.float32)
    member = jnp.zeros((n_tok, rows), jnp.float32)
    for k in range(n_top):
        r = routes[:, k : k + 1]
        dense = dense + jnp.where(lane == r, gates[:, k : k + 1], 0.0)
        member = jnp.where((r >= (m // piece) * EXP_MESH) & (r < (m // piece + 1) * EXP_MESH), 1.0, member)
    chosen = jnp.where(t // block == lax.rem(m, piece), member, 0.0)
    for j in range(n_local):
        stage[j, :, :chunk] = tok_ref[:, j * chunk : (j + 1) * chunk]
        stage[j, :, chunk : chunk + LANES] = dense.astype(jnp.bfloat16)
        stage[j, :, chunk + LANES :] = chosen.astype(jnp.bfloat16)
    recv_a[me] = stage[me]

    pl.semaphore_wait(barrier, n_local - 1 + n_group - 1)

    sends = []
    for k in range(1, n_local):
        to = lax.rem(me + k, n_local)
        copy = pltpu.make_async_remote_copy(
            src_ref=stage.at[to],
            dst_ref=recv_a.at[me],
            send_sem=a_send.at[k],
            recv_sem=a_recv.at[k],
            device_id={"local": to},
            device_id_type=pl.DeviceIdType.MESH,
        )
        copy.start()
        sends.append(copy)
    for copy in sends:
        copy.wait_recv()

    got = jnp.concatenate([recv_a[j].astype(jnp.float32) for j in range(n_local)], axis=0).astype(jnp.bfloat16)
    packed = lax.dot_general(
        got[:, chunk + LANES :],
        got[:, : chunk + LANES],
        (((0,), (0,)), ((), ())),
        preferred_element_type=jnp.float32,
    ).astype(jnp.bfloat16)
    send_b[...] = packed.reshape(n_group, piece, chunk + LANES)

    partners = range(1, n_group)
    for k in partners:
        to = flip(g, k)
        copy = pltpu.make_async_remote_copy(
            src_ref=send_b.at[to],
            dst_ref=x0.at[g],
            send_sem=b_send.at[k],
            recv_sem=b_recv.at[k],
            device_id={"group": to},
            device_id_type=pl.DeviceIdType.MESH,
        )
        copy.start()
        sends.append(copy)
    x0[g] = send_b[g]

    def onward(src, dst, at, send, recv, to):
        copy = pltpu.make_async_remote_copy(
            src_ref=src,
            dst_ref=dst.at[at],
            send_sem=send,
            recv_sem=recv,
            device_id={"local": to},
            device_id_type=pl.DeviceIdType.MESH,
        )
        copy.start()
        sends.append(copy)
        return copy

    order = range(n_group)
    b_copy = dict(zip(partners, sends[n_local - 1 :]))
    core_in, y_in, diag_in = [], [], []

    def forward(step):
        at = flip(g, order[step])
        y_in[step].wait_recv()
        diag_in.append(onward(x2.at[at], x3, at, c_send.at[2, step], x3_recv.at[step], l_core))

    lag = 6
    for step, k in enumerate(order):
        if k:
            b_copy[k].wait_recv()
        at = flip(g, k)
        src = x0.at[at, :, pl.ds(0, chunk)]
        y_in.append(onward(src, x2, at, c_send.at[1, step], x2_recv.at[step], l_y))
        core_in.append(onward(src, x1, at, c_send.at[0, step], x1_recv.at[step], l_core))
        if step >= lag:
            forward(step - lag)

    def rows_of(x):
        return x[:, :, :chunk].reshape(rows, chunk)

    def add(slot, x, first=False):
        for load in loads[2 * slot : 2 * slot + 2]:
            load.wait()
        a = rows_of(x)
        for w, acc in ((wg, acc_g), (wu, acc_u)):
            p = jnp.dot(a, w[slot], preferred_element_type=jnp.float32)
            acc[...] = p if first else acc[...] + p

    add(0, x0, True)
    for step in range(n_group - lag, n_group):
        forward(step)
    for copy in core_in:
        copy.wait_recv()
    add(1, x1)
    add(2, x2)
    for copy in diag_in:
        copy.wait_recv()
    for load in loads[6:8]:
        load.wait()

    expert = g * EXP_MESH + me // (n_local // EXP_MESH)
    gate_rows = x0[:, :, chunk:].reshape(rows, LANES).astype(jnp.float32)
    mine = lax.broadcasted_iota(jnp.int32, (rows, LANES), 1) == expert
    scale = jnp.sum(jnp.where(mine, gate_rows, 0.0), axis=1, keepdims=True)
    a = rows_of(x3)
    width = 256
    for n in range(0, out_ref.shape[2], width):
        at = slice(n, n + width)
        pg = acc_g[:, at] + jnp.dot(a, wg[3, :, at], preferred_element_type=jnp.float32)
        pu = acc_u[:, at] + jnp.dot(a, wu[3, :, at], preferred_element_type=jnp.float32)
        out_ref[0, :, at] = (pg / (1.0 + jnp.exp(-pg)) * pu * scale).astype(jnp.bfloat16)

    for copy in sends:
        copy.wait_send()


def fused(tokens, routes, route_gates, gate_weight, up_weight):
    n_group, n_local = lax.axis_size("group"), lax.axis_size("local")
    n_tok, depth = tokens.shape
    hidden = gate_weight.shape[-1]
    chunk = depth // n_local
    piece = n_local * n_tok // block_tokens(n_group)
    rows = n_group * piece
    bf16, f32 = jnp.bfloat16, jnp.float32
    vmem = pl.BlockSpec(memory_space=pltpu.VMEM)
    hbm = pl.BlockSpec(memory_space=pl.ANY)
    dma = pltpu.SemaphoreType.DMA
    return pl.pallas_call(
        functools.partial(kernel, n_group, n_local),
        out_shape=jax.ShapeDtypeStruct((1, rows, hidden), bf16),
        in_specs=[hbm] * 5,
        out_specs=vmem,
        scratch_shapes=[
            pltpu.VMEM(tokens.shape, tokens.dtype),
            pltpu.VMEM(routes.shape, routes.dtype),
            pltpu.VMEM(route_gates.shape, route_gates.dtype),
            pltpu.VMEM((n_local, n_tok, chunk + LANES + rows), bf16),
            pltpu.VMEM((n_local, n_tok, chunk + LANES + rows), bf16),
            pltpu.VMEM((n_group, piece, chunk + LANES), bf16),
            pltpu.VMEM((n_group, piece, chunk + LANES), bf16),
            pltpu.VMEM((n_group, piece, chunk), bf16),
            pltpu.VMEM((n_group, piece, chunk), bf16),
            pltpu.VMEM((n_group, piece, chunk), bf16),
            pltpu.VMEM((n_local, chunk, hidden), bf16),
            pltpu.VMEM((n_local, chunk, hidden), bf16),
            pltpu.VMEM((rows, hidden), f32),
            pltpu.VMEM((rows, hidden), f32),
            dma((3,)),
            dma((n_local, 2)),
            dma((n_local,)),
            dma((n_local,)),
            dma((n_group,)),
            dma((n_group,)),
            dma((3, n_group)),
            dma((n_group,)),
            dma((n_group,)),
            dma((n_group,)),
        ],
        compiler_params=pltpu.CompilerParams(
            collective_id=0, has_side_effects=True, vmem_limit_bytes=48 * 1024 * 1024
        ),
        cost_estimate=pl.CostEstimate(
            flops=4 * rows * depth * hidden,
            bytes_accessed=4 * depth * hidden + 2 * rows * hidden,
            transcendentals=rows * hidden,
        ),
    )(tokens, routes, route_gates, gate_weight, up_weight)


def staged(tokens, routes, route_gates, gate_weight, up_weight):
    n_group, n_local = lax.axis_size("group"), lax.axis_size("local")
    block = block_tokens(n_group)
    n_tok, depth = tokens.shape
    groups = jnp.arange(n_group, dtype=jnp.int32)
    member = jnp.any((routes // EXP_MESH)[:, :, None] == groups, axis=1).astype(jnp.bfloat16)
    packed = jnp.einsum(
        "ibg,ibd->gid",
        member.reshape(-1, block, n_group),
        tokens.reshape(-1, block, depth),
        preferred_element_type=jnp.float32,
    ).astype(jnp.bfloat16)
    experts = groups[:, None] * EXP_MESH + jnp.arange(EXP_MESH, dtype=jnp.int32)
    matches = (routes[:, :, None, None] == experts).astype(jnp.float32)
    dense = jnp.sum(route_gates[:, :, None, None] * matches, axis=1)
    gates = dense.reshape(-1, block, n_group, EXP_MESH).sum(axis=1).transpose(1, 0, 2).astype(jnp.bfloat16)

    def over(x):
        x = lax.all_to_all(x, "group", split_axis=0, concat_axis=0, tiled=True)
        x = lax.all_gather(x, "local", axis=1, tiled=True)
        return x.reshape(-1, x.shape[-1])

    x, scales = over(packed), over(gates).astype(jnp.float32)
    slot = lax.axis_index("local") // (n_local // EXP_MESH)
    mine = (jnp.arange(EXP_MESH, dtype=jnp.int32) == slot).astype(jnp.float32)
    scale = jnp.sum(scales * mine, axis=-1)[:, None]
    pre_gate = jnp.dot(x, gate_weight[0], preferred_element_type=jnp.float32)
    pre_up = jnp.dot(x, up_weight[0], preferred_element_type=jnp.float32)
    return (jax.nn.silu(pre_gate) * pre_up * scale).astype(jnp.bfloat16)[None]


def shards(tokens, routes, route_gates, gate_weight, up_weight):
    n_group, n_local = lax.axis_size("group"), lax.axis_size("local")
    piece = n_local * tokens.shape[0] // block_tokens(n_group)
    fits = (
        n_local == 2 * CORES
        and n_group & (n_group - 1) == 0
        and n_local % EXP_MESH == 0
        and tokens.shape[1] % (n_local * LANES) == 0
        and piece % ROW_TILE == 0
        and (n_group * piece) % LANES == 0
        and n_group * EXP_MESH <= LANES
        and gate_weight.shape[-1] % 256 == 0
    )
    plan = fused if fits else staged
    return plan(tokens, routes, route_gates, gate_weight, up_weight)


def solution(mesh):
    rows = P(("group", "local"), None)
    blocks = P(("group", "local"), None, None)
    return jax.shard_map(
        shards, mesh=mesh, in_specs=(rows, rows, rows, blocks, blocks), out_specs=blocks, check_vma=False
    )
```

```python
import functools

import jax
import jax.numpy as jnp
from jax import lax
from jax.experimental import pallas as pl
from jax.experimental.pallas import tpu as pltpu
from jax.sharding import PartitionSpec as P

NEG = 8
EXP_MESH = 4
TOPG = 4
TOP = 8
LANES = 128
ROW_TILE = 16
CORES = 2


def block_tokens(n_group):
    return n_group // (TOPG * min(TOP // TOPG, n_group // NEG))


def flip(index, bits):
    bit = 1
    while bit <= bits:
        if bits & bit:
            index = index + bit * (1 - 2 * lax.rem(index // bit, 2))
        bit *= 2
    return index


def kernel(
    n_group,
    n_local,
    tok_hbm,
    rt_hbm,
    ga_hbm,
    gw_hbm,
    uw_hbm,
    out_ref,
    tok_ref,
    rt_ref,
    ga_ref,
    stage,
    recv_a,
    send_b,
    x0,
    x1,
    x2,
    x3,
    wg,
    wu,
    acc_g,
    acc_u,
    in_sem,
    w_sem,
    a_send,
    a_recv,
    b_send,
    b_recv,
    c_send,
    x1_recv,
    x2_recv,
    x3_recv,
    v_out,
    v_in,
    v_send,
    v_recv,
):
    g = lax.axis_index("group")
    me = lax.axis_index("local")
    n_tok, depth = tok_ref.shape
    chunk = depth // n_local
    block = block_tokens(n_group)
    piece = n_local * n_tok // block
    rows = n_group * piece
    n_top = rt_ref.shape[1]

    core = lax.rem(me, CORES)
    l_core = me + 1 - 2 * core
    l_y = lax.rem(me + CORES, n_local)
    l_diag = lax.rem(l_core + CORES, n_local)

    small = []
    for i, (src, dst) in enumerate(((tok_hbm, tok_ref), (rt_hbm, rt_ref), (ga_hbm, ga_ref))):
        small.append(pltpu.make_async_copy(src, dst, in_sem.at[i]))
        small[-1].start()

    barrier = pltpu.get_barrier_semaphore()
    for k in range(1, n_local):
        pl.semaphore_signal(
            barrier, inc=1, device_id={"local": lax.rem(me + k, n_local)}, device_id_type=pl.DeviceIdType.MESH
        )
    for k in range(1, n_group):
        pl.semaphore_signal(
            barrier, inc=1, device_id={"group": flip(g, k)}, device_id_type=pl.DeviceIdType.MESH
        )

    loads = []
    for slot, part in enumerate((me, l_core, l_y, l_diag)):
        at = pl.ds(pl.multiple_of(part * chunk, LANES), chunk)
        for i, (src, dst) in enumerate(((gw_hbm, wg), (uw_hbm, wu))):
            load = pltpu.make_async_copy(src.at[0, at, :], dst.at[slot], w_sem.at[slot, i])
            load.start()
            loads.append(load)

    for copy in small:
        copy.wait()
    lane = lax.broadcasted_iota(jnp.int32, (n_tok, LANES), 1)
    m = lax.broadcasted_iota(jnp.int32, (n_tok, rows), 1)
    t = lax.broadcasted_iota(jnp.int32, (n_tok, rows), 0) + me * n_tok
    routes = rt_ref[...]
    gates = ga_ref[...]
    dense = jnp.zeros((n_tok, LANES), jnp.float32)
    member = jnp.zeros((n_tok, rows), jnp.float32)
    for k in range(n_top):
        r = routes[:, k : k + 1]
        dense = dense + jnp.where(lane == r, gates[:, k : k + 1], 0.0)
        member = jnp.where((r >= (m // piece) * EXP_MESH) & (r < (m // piece + 1) * EXP_MESH), 1.0, member)
    chosen = jnp.where(t // block == lax.rem(m, piece), member, 0.0)
    for j in range(n_local):
        stage[j, :, :chunk] = tok_ref[:, j * chunk : (j + 1) * chunk]
        stage[j, :, chunk : chunk + LANES] = dense.astype(jnp.bfloat16)
        stage[j, :, chunk + LANES :] = chosen.astype(jnp.bfloat16)
    recv_a[me] = stage[me]

    pl.semaphore_wait(barrier, n_local - 1 + n_group - 1)

    sends = []
    for k in range(1, n_local):
        to = lax.rem(me + k, n_local)
        copy = pltpu.make_async_remote_copy(
            src_ref=stage.at[to],
            dst_ref=recv_a.at[me],
            send_sem=a_send.at[k],
            recv_sem=a_recv.at[k],
            device_id={"local": to},
            device_id_type=pl.DeviceIdType.MESH,
        )
        copy.start()
        sends.append(copy)
    for copy in sends:
        copy.wait_recv()

    got = jnp.concatenate([recv_a[j].astype(jnp.float32) for j in range(n_local)], axis=0).astype(jnp.bfloat16)
    packed = lax.dot_general(
        got[:, chunk + LANES :],
        got[:, : chunk + LANES],
        (((0,), (0,)), ((), ())),
        preferred_element_type=jnp.float32,
    )
    send_b[...] = packed[:, :chunk].astype(jnp.bfloat16).reshape(n_group, piece, chunk)

    partners = range(1, n_group)
    for k in partners:
        to = flip(g, k)
        copy = pltpu.make_async_remote_copy(
            src_ref=send_b.at[to],
            dst_ref=x0.at[g],
            send_sem=b_send.at[k],
            recv_sem=b_recv.at[k],
            device_id={"group": to},
            device_id_type=pl.DeviceIdType.MESH,
        )
        copy.start()
        sends.append(copy)
    x0[g] = send_b[g]

    row = lax.broadcasted_iota(jnp.int32, (rows, LANES), 0)
    col = lax.broadcasted_iota(jnp.int32, (rows, LANES), 1)
    slot = me // (n_local // EXP_MESH)
    hers = jnp.where(col == (row // piece) * EXP_MESH + slot, packed[:, chunk:], 0.0)
    hers = jnp.sum(hers, axis=1, keepdims=True)
    place = lax.broadcasted_iota(jnp.int32, (rows, rows), 1)
    from_row = lax.broadcasted_iota(jnp.int32, (rows, rows), 0)
    spread = jnp.where(place == g * piece + lax.rem(from_row, piece), hers, 0.0)
    v_out[...] = jnp.sum(spread.reshape(n_group, piece, rows), axis=1).reshape(n_group, 1, rows)
    gate_in = []
    for k in partners:
        to = flip(g, k)
        copy = pltpu.make_async_remote_copy(
            src_ref=v_out.at[to],
            dst_ref=v_in.at[g],
            send_sem=v_send.at[k],
            recv_sem=v_recv.at[k],
            device_id={"group": to},
            device_id_type=pl.DeviceIdType.MESH,
        )
        copy.start()
        gate_in.append(copy)
    v_in[g] = v_out[g]

    def onward(src, dst, at, send, recv, to):
        copy = pltpu.make_async_remote_copy(
            src_ref=src,
            dst_ref=dst.at[at],
            send_sem=send,
            recv_sem=recv,
            device_id={"local": to},
            device_id_type=pl.DeviceIdType.MESH,
        )
        copy.start()
        sends.append(copy)
        return copy

    order = range(n_group)
    b_copy = dict(zip(partners, sends[n_local - 1 :]))
    core_in, y_in, diag_in = [], [], []

    def forward(step):
        at = flip(g, order[step])
        y_in[step].wait_recv()
        diag_in.append(onward(x2.at[at], x3, at, c_send.at[2, step], x3_recv.at[step], l_core))

    lag = 6
    for step, k in enumerate(order):
        if k:
            b_copy[k].wait_recv()
        at = flip(g, k)
        src = x0.at[at]
        y_in.append(onward(src, x2, at, c_send.at[1, step], x2_recv.at[step], l_y))
        core_in.append(onward(src, x1, at, c_send.at[0, step], x1_recv.at[step], l_core))
        if step >= lag:
            forward(step - lag)

    def rows_of(x):
        return x[...].reshape(rows, chunk)

    def add(slot, x, first=False):
        for load in loads[2 * slot : 2 * slot + 2]:
            load.wait()
        a = rows_of(x)
        for w, acc in ((wg, acc_g), (wu, acc_u)):
            p = jnp.dot(a, w[slot], preferred_element_type=jnp.float32)
            acc[...] = p if first else acc[...] + p

    add(0, x0, True)
    for step in range(n_group - lag, n_group):
        forward(step)
    for copy in core_in:
        copy.wait_recv()
    add(1, x1)
    add(2, x2)
    for copy in diag_in:
        copy.wait_recv()
    for load in loads[6:8]:
        load.wait()

    for copy in gate_in:
        copy.wait_recv()
    whole = jnp.sum(v_in[...].reshape(n_group, rows), axis=0, keepdims=True)
    scale = jnp.sum(jnp.where(place == from_row, whole, 0.0), axis=1, keepdims=True)
    a = rows_of(x3)
    width = 256
    for n in range(0, out_ref.shape[2], width):
        at = slice(n, n + width)
        pg = acc_g[:, at] + jnp.dot(a, wg[3, :, at], preferred_element_type=jnp.float32)
        pu = acc_u[:, at] + jnp.dot(a, wu[3, :, at], preferred_element_type=jnp.float32)
        out_ref[0, :, at] = (pg / (1.0 + jnp.exp(-pg)) * pu * scale).astype(jnp.bfloat16)

    for copy in sends + gate_in:
        copy.wait_send()


def fused(tokens, routes, route_gates, gate_weight, up_weight):
    n_group, n_local = lax.axis_size("group"), lax.axis_size("local")
    n_tok, depth = tokens.shape
    hidden = gate_weight.shape[-1]
    chunk = depth // n_local
    piece = n_local * n_tok // block_tokens(n_group)
    rows = n_group * piece
    bf16, f32 = jnp.bfloat16, jnp.float32
    vmem = pl.BlockSpec(memory_space=pltpu.VMEM)
    hbm = pl.BlockSpec(memory_space=pl.ANY)
    dma = pltpu.SemaphoreType.DMA
    return pl.pallas_call(
        functools.partial(kernel, n_group, n_local),
        out_shape=jax.ShapeDtypeStruct((1, rows, hidden), bf16),
        in_specs=[hbm] * 5,
        out_specs=vmem,
        scratch_shapes=[
            pltpu.VMEM(tokens.shape, tokens.dtype),
            pltpu.VMEM(routes.shape, routes.dtype),
            pltpu.VMEM(route_gates.shape, route_gates.dtype),
            pltpu.VMEM((n_local, n_tok, chunk + LANES + rows), bf16),
            pltpu.VMEM((n_local, n_tok, chunk + LANES + rows), bf16),
            pltpu.VMEM((n_group, piece, chunk), bf16),
            pltpu.VMEM((n_group, piece, chunk), bf16),
            pltpu.VMEM((n_group, piece, chunk), bf16),
            pltpu.VMEM((n_group, piece, chunk), bf16),
            pltpu.VMEM((n_group, piece, chunk), bf16),
            pltpu.VMEM((n_local, chunk, hidden), bf16),
            pltpu.VMEM((n_local, chunk, hidden), bf16),
            pltpu.VMEM((rows, hidden), f32),
            pltpu.VMEM((rows, hidden), f32),
            dma((3,)),
            dma((n_local, 2)),
            dma((n_local,)),
            dma((n_local,)),
            dma((n_group,)),
            dma((n_group,)),
            dma((3, n_group)),
            dma((n_group,)),
            dma((n_group,)),
            dma((n_group,)),
            pltpu.VMEM((n_group, 1, rows), f32),
            pltpu.VMEM((n_group, 1, rows), f32),
            dma((n_group,)),
            dma((n_group,)),
        ],
        compiler_params=pltpu.CompilerParams(
            collective_id=0, has_side_effects=True, vmem_limit_bytes=48 * 1024 * 1024
        ),
        cost_estimate=pl.CostEstimate(
            flops=4 * rows * depth * hidden,
            bytes_accessed=4 * depth * hidden + 2 * rows * hidden,
            transcendentals=rows * hidden,
        ),
    )(tokens, routes, route_gates, gate_weight, up_weight)


def staged(tokens, routes, route_gates, gate_weight, up_weight):
    n_group, n_local = lax.axis_size("group"), lax.axis_size("local")
    block = block_tokens(n_group)
    n_tok, depth = tokens.shape
    groups = jnp.arange(n_group, dtype=jnp.int32)
    member = jnp.any((routes // EXP_MESH)[:, :, None] == groups, axis=1).astype(jnp.bfloat16)
    packed = jnp.einsum(
        "ibg,ibd->gid",
        member.reshape(-1, block, n_group),
        tokens.reshape(-1, block, depth),
        preferred_element_type=jnp.float32,
    ).astype(jnp.bfloat16)
    experts = groups[:, None] * EXP_MESH + jnp.arange(EXP_MESH, dtype=jnp.int32)
    matches = (routes[:, :, None, None] == experts).astype(jnp.float32)
    dense = jnp.sum(route_gates[:, :, None, None] * matches, axis=1)
    gates = dense.reshape(-1, block, n_group, EXP_MESH).sum(axis=1).transpose(1, 0, 2).astype(jnp.bfloat16)

    def over(x):
        x = lax.all_to_all(x, "group", split_axis=0, concat_axis=0, tiled=True)
        x = lax.all_gather(x, "local", axis=1, tiled=True)
        return x.reshape(-1, x.shape[-1])

    x, scales = over(packed), over(gates).astype(jnp.float32)
    slot = lax.axis_index("local") // (n_local // EXP_MESH)
    mine = (jnp.arange(EXP_MESH, dtype=jnp.int32) == slot).astype(jnp.float32)
    scale = jnp.sum(scales * mine, axis=-1)[:, None]
    pre_gate = jnp.dot(x, gate_weight[0], preferred_element_type=jnp.float32)
    pre_up = jnp.dot(x, up_weight[0], preferred_element_type=jnp.float32)
    return (jax.nn.silu(pre_gate) * pre_up * scale).astype(jnp.bfloat16)[None]


def shards(tokens, routes, route_gates, gate_weight, up_weight):
    n_group, n_local = lax.axis_size("group"), lax.axis_size("local")
    piece = n_local * tokens.shape[0] // block_tokens(n_group)
    fits = (
        n_local == 2 * CORES
        and n_group & (n_group - 1) == 0
        and n_local % EXP_MESH == 0
        and tokens.shape[1] % (n_local * LANES) == 0
        and piece % ROW_TILE == 0
        and (n_group * piece) % LANES == 0
        and n_group * EXP_MESH <= LANES
        and gate_weight.shape[-1] % 256 == 0
    )
    plan = fused if fits else staged
    return plan(tokens, routes, route_gates, gate_weight, up_weight)


def solution(mesh):
    rows = P(("group", "local"), None)
    blocks = P(("group", "local"), None, None)
    return jax.shard_map(
        shards, mesh=mesh, in_specs=(rows, rows, rows, blocks, blocks), out_specs=blocks, check_vma=False
    )
```
